128 devices in a mesh: dp: 128 (over x, z, y, core).
Axes of the slice: x: 4, y: 4, z: 4, core: 2. Of those that a mesh axis runs over, the one named last changes fastest.
Arguments:
- grad: float32 [4096, 8192], P('dp'), may hold values from -8 to 8
- block_owner: int32 [128], replicated, may hold values from 0 to 127, as said below
- left_factor: float32 [256, 512, 512], P('dp'), may hold values from -3 to 3
- right_factor: float32 [256, 512, 512], P('dp'), may hold values from -3 to 3
- left_basis: float32 [256, 512, 512], P('dp'), may hold values from -0.25 to 0.25
- right_basis: float32 [256, 512, 512], P('dp'), may hold values from -0.25 to 0.25
- first_moment: float32 [256, 512, 512], P('dp'), may hold values from -0.072 to 0.072
- second_moment: float32 [256, 512, 512], P('dp'), may hold values from 0.0002 to 0.002
Outputs:
- updates: bfloat16 [4096, 8192], P('dp')
- new_left: float32 [256, 512, 512], P('dp')
- new_right: float32 [256, 512, 512], P('dp')
- new_first: float32 [256, 512, 512], P('dp')
- new_second: float32 [256, 512, 512], P('dp')
The draws below stay inside these ranges and needn't reach their ends.
Inputs may be any that keep to these rules, and one draw needn't show every extreme that they name: `block_owner`: block b covers rows 512 * (b // 16) to 512 * (b // 16) + 511 of the stacked matrices. The 16 blocks of one row of blocks have different owners. A quarter of the devices own 2 blocks each, half own one block and the rest own none.
All inputs are finite; a program needn't handle non-finite values.
Results may differ from the reference program's by a relative error of at most 0.001.
Values may be sent and summed in bfloat16 or wider, within the bound.
A program may use at most 128 MiB of HBM per device.

```python
import math
import jax
import jax.numpy as jnp
from jax import lax

W = 8192
B = 512
CAP = 2
BLOCKS = 128
CB = 16
ROWS = 4096
N_DP = 128


def draw_grad(key, part):
    key = jax.random.fold_in(key, 5)
    key_noise, key_rows, key_cols = jax.random.split(key, 3)
    row_pos = jnp.arange(ROWS, dtype=jnp.float32) / float(ROWS - 1)
    row_scale = jnp.exp(jax.random.uniform(key_rows, (ROWS,), jnp.float32, math.log(0.5), math.log(5.0)))
    col_scale = jnp.exp(jax.random.uniform(key_cols, (W,), jnp.float32, math.log(0.5), math.log(5.0)))
    values = jnp.clip(jax.random.normal(key_noise, (ROWS, W), jnp.float32), -4.0, 4.0)
    rise = jnp.sqrt(1.0 + 2.0 * row_pos)
    return 0.02 * values * (row_scale * rise)[:, None] * col_scale[None, :]


def draw_block_owner(key, part):
    key = jax.random.fold_in(key, 9)
    key_dev, key_grp, key_col = jax.random.split(key, 3)
    ranked = jax.random.permutation(key_dev, N_DP).astype(jnp.int32)
    tokens = jnp.arange(BLOCKS, dtype=jnp.int32)
    half_count = BLOCKS // 2
    quarter = N_DP // 4
    which = jnp.where(tokens < half_count, tokens // 2, quarter + tokens - half_count)
    owners = ranked[which]
    groups = BLOCKS // CB
    group_perm = jax.random.permutation(key_grp, groups).astype(jnp.int32)
    group_of = group_perm[tokens % groups]
    col_keys = jax.random.split(key_col, groups)

    def column_order(one_key):
        return jax.random.permutation(one_key, CB).astype(jnp.int32)
    col_table = jax.vmap(column_order)(col_keys)
    column = col_table[group_of, tokens // groups]
    place = group_of * CB + column
    return jnp.zeros((BLOCKS,), jnp.int32).at[place].set(owners)


def level_of(rng, extent, cuts, least, top_value):
    gain = 1.0
    for position, shards_of in cuts:
        draws = jax.random.uniform(jax.random.fold_in(jax.random.fold_in(rng, 6), position), (shards_of,), jnp.float32, least / len(cuts), top_value / len(cuts))
        gain = gain * jnp.repeat(jnp.exp(draws), extent[position] // shards_of).reshape((-1,) + (1,) * (len(extent) - 1 - position))
    return gain


def bell_draw(key, dims, deviation, bound, pieces=(), held_as=jnp.bfloat16):
    values = jax.random.normal(key, dims, jnp.float32) * deviation
    if len(pieces) > 0:
        values = level_of(key, dims, pieces, -0.22, 0.18) * values
    return jnp.clip(values, min=-bound, max=bound).astype(held_as)


def setup_inputs(seed: int = 0) -> dict:
    splits = jax.random.split(jax.random.key(seed), 9)
    return {
        "grad": draw_grad(jax.random.fold_in(splits[8], 71), 0),
        "block_owner": draw_block_owner(jax.random.fold_in(splits[8], 71), 0),
        "left_factor": bell_draw(splits[2], (N_DP * CAP, B, B), 0.5, 3.0, ((0, 128),), jnp.float32),
        "right_factor": bell_draw(splits[3], (N_DP * CAP, B, B), 0.5, 3.0, ((0, 128),), jnp.float32),
        "left_basis": bell_draw(splits[4], (N_DP * CAP, B, B), B ** -0.5, 0.25, ((0, 128),), jnp.float32),
        "right_basis": bell_draw(splits[5], (N_DP * CAP, B, B), B ** -0.5, 0.25, ((0, 128),), jnp.float32),
        "first_moment": bell_draw(splits[6], (N_DP * CAP, B, B), 0.012, 0.072, ((0, 128),), jnp.float32),
        "second_moment": jnp.clip(jnp.exp(math.log(0.002) - 2.3025852 * jax.random.uniform(splits[7], (N_DP * CAP, B, B), jnp.float32) ** level_of(splits[7], (N_DP * CAP, B, B), ((0, 128),), -0.2, 0.2)), 0.0002, 0.002),
    }


full_precision = lax.Precision.HIGHEST
first_correction = 1.0 - 0.9 ** 10
second_correction = 1.0 - 0.95 ** 10

def matmul_full(left_arr, right_arr):
    return jnp.dot(left_arr, right_arr, precision=full_precision)

def block_slots(block_owner):
    count = block_owner.shape[0]
    positions = jnp.arange(count, dtype=jnp.int32)
    same_owner = block_owner[:, None] == block_owner[None, :]
    earlier = positions[None, :] < positions[:, None]
    return lax.optimization_barrier(jnp.sum(jnp.where(same_owner & earlier, 1, 0), axis=1)).astype(jnp.int32)

def soap_block(grad_block, left_stat, right_stat, left_rot, right_rot, first_stat, second_stat):
    next_left = 0.95 * left_stat + 0.05 * matmul_full(grad_block, grad_block.T)
    next_right = 0.95 * right_stat + 0.05 * matmul_full(grad_block.T, grad_block)
    rotated = matmul_full(matmul_full(left_rot.T, grad_block), right_rot)
    next_first = 0.9 * first_stat + 0.1 * rotated
    next_second = 0.95 * second_stat + 0.05 * rotated * rotated
    direction = next_first / first_correction / (jnp.sqrt(next_second / second_correction) + 1e-08)
    update = matmul_full(matmul_full(left_rot, direction), right_rot.T).astype(jnp.bfloat16)
    return (next_left, next_right, next_first, next_second, update)

def reference(grad, block_owner, left_factor, right_factor, left_basis, right_basis, first_moment, second_moment):
    sum_squares = jnp.sum(grad * grad)
    scale = jnp.minimum(1.0, 0.04 / (jnp.sqrt(sum_squares / (ROWS * W)) + 1e-06))
    clipped = grad * scale
    groups = BLOCKS // CB
    blocks = clipped.reshape(groups, B, CB, B).transpose(0, 2, 1, 3).reshape(BLOCKS, B, B)
    target = (CAP * block_owner + block_slots(block_owner)).astype(jnp.int32)

    def one_block(packed):
        grad_block, state_index = packed
        return soap_block(grad_block, left_factor[state_index], right_factor[state_index], left_basis[state_index], right_basis[state_index], first_moment[state_index], second_moment[state_index])
    next_left, next_right, next_first, next_second, update = lax.map(one_block, (blocks, target))
    updates = update.reshape(groups, CB, B, B).transpose(0, 2, 1, 3).reshape(ROWS, W)
    return (updates, left_factor.at[target].set(next_left), right_factor.at[target].set(next_right), first_moment.at[target].set(next_first), second_moment.at[target].set(next_second))
```

```python
import jax
import jax.numpy as jnp
from jax import lax
from jax.experimental import pallas as pl
from jax.experimental.pallas import tpu as pltpu
from jax.sharding import PartitionSpec as P

MESH = pl.DeviceIdType.MESH
N = 128


def shift_peer(me, k):
    x, z, y, c = me // 32, (me // 8) % 4, (me // 2) % 4, me % 2
    dx, dz, dy, dc = k % 4, (k // 4) % 4, (k // 16) % 4, k // 64
    return ((x + dx) % 4) * 32 + ((z + dz) % 4) * 8 + ((y + dy) % 4) * 2 + (c + dc) % 2


def enter(me):
    barrier = pltpu.get_barrier_semaphore()

    def hail(k, carry):
        pl.semaphore_signal(barrier, inc=1, device_id=(shift_peer(me, k),), device_id_type=MESH)
        return carry

    lax.fori_loop(1, N, hail, 0)
    return barrier


def forward_kernel(index_ref, grad_ref, out_ref, send1, recv1, send2, sems):
    me = lax.axis_index("dp")
    group, rank = me // 16, me % 16
    half, part = group // 4, group % 4
    barrier = enter(me)
    for h in range(2):
        for j in range(4):
            for c in range(16):
                send1[h * 4 + j, c] = grad_ref[16 * h:16 * h + 16, 512 * c + 128 * j:512 * c + 128 * j + 128]
    pl.semaphore_wait(barrier, N - 1)

    def spread(d, carry):
        to = (group + d) % 8
        pltpu.make_async_remote_copy(
            src_ref=send1.at[to], dst_ref=recv1.at[group], send_sem=sems.at[0], recv_sem=sems.at[1],
            device_id=(to * 16 + rank,), device_id_type=MESH).start()
        return carry

    lax.fori_loop(1, 8, spread, 0)
    pltpu.make_async_copy(send1.at[group], recv1.at[group], sems.at[1]).start()
    pltpu.make_async_copy(recv1, recv1, sems.at[1]).wait()

    def pack(o):
        for s in range(2):
            b = index_ref[2 * o + s]
            send2[o, s] = recv1[b // 16, b % 16]

    row = pl.multiple_of(32 * rank + 16 * half, 16)
    col = pl.multiple_of(128 * part, 128)
    place = out_ref.at[:, pl.ds(row, 16), pl.ds(col, 128)]

    def deliver(k, carry):
        o = shift_peer(me, k)
        pack(o)
        pltpu.make_async_remote_copy(
            src_ref=send2.at[o], dst_ref=place, send_sem=sems.at[2], recv_sem=sems.at[3],
            device_id=(o,), device_id_type=MESH).start()
        return carry

    lax.fori_loop(1, N, deliver, 0)
    pack(me)
    pltpu.make_async_copy(send2.at[me], place, sems.at[3]).start()
    pltpu.make_async_copy(out_ref, out_ref, sems.at[3]).wait()
    pltpu.make_async_copy(send1.at[pl.ds(0, 7)], send1.at[pl.ds(0, 7)], sems.at[0]).wait()
    pltpu.make_async_copy(send2.at[pl.ds(0, N - 1)], send2.at[pl.ds(0, N - 1)], sems.at[2]).wait()


def forward(index, grad):
    dt = grad.dtype
    return pl.pallas_call(
        forward_kernel,
        out_shape=jax.ShapeDtypeStruct((2, 512, 512), dt),
        in_specs=[pl.BlockSpec(memory_space=pltpu.SMEM), pl.BlockSpec(memory_space=pltpu.VMEM)],
        out_specs=pl.BlockSpec(memory_space=pltpu.VMEM),
        scratch_shapes=[
            pltpu.VMEM((8, 16, 16, 128), dt),
            pltpu.VMEM((8, 16, 16, 128), dt),
            pltpu.VMEM((N, 2, 16, 128), dt),
            pltpu.SemaphoreType.DMA((4,)),
        ],
        compiler_params=pltpu.CompilerParams(
            collective_id=0, has_side_effects=True, vmem_limit_bytes=40 * 2**20),
        name="forward_rows",
    )(index, grad)


def back_kernel(index_ref, upd_ref, out_ref, recv2, send1, recv1, sems):
    me = lax.axis_index("dp")
    group, rank = me // 16, me % 16
    barrier = enter(me)
    pl.semaphore_wait(barrier, N - 1)

    def place(i):
        g = i // 16
        row = pl.multiple_of(32 * (i % 16) + 16 * (g // 4), 16)
        col = pl.multiple_of(128 * (g % 4), 128)
        return upd_ref.at[:, pl.ds(row, 16), pl.ds(col, 128)]

    def deliver(k, carry):
        o = shift_peer(me, k)
        pltpu.make_async_remote_copy(
            src_ref=place(o), dst_ref=recv2.at[me], send_sem=sems.at[0], recv_sem=sems.at[1],
            device_id=(o,), device_id_type=MESH).start()
        return carry

    lax.fori_loop(1, N, deliver, 0)
    pltpu.make_async_copy(place(me), recv2.at[me], sems.at[1]).start()
    pltpu.make_async_copy(recv2, recv2, sems.at[1]).wait()

    def pack(g):
        for c in range(16):
            q = index_ref[16 * g + c]
            send1[g, c] = recv2[q // 2, q % 2]

    def spread(d, carry):
        to = (group + d) % 8
        pack(to)
        pltpu.make_async_remote_copy(
            src_ref=send1.at[to], dst_ref=recv1.at[group], send_sem=sems.at[2], recv_sem=sems.at[3],
            device_id=(to * 16 + rank,), device_id_type=MESH).start()
        return carry

    lax.fori_loop(1, 8, spread, 0)
    pack(group)
    pltpu.make_async_copy(send1.at[group], recv1.at[group], sems.at[3]).start()
    pltpu.make_async_copy(recv1, recv1, sems.at[3]).wait()
    for h in range(2):
        for j in range(4):
            for c in range(16):
                out_ref[16 * h:16 * h + 16, 512 * c + 128 * j:512 * c + 128 * j + 128] = recv1[h * 4 + j, c]
    pltpu.make_async_copy(recv2.at[pl.ds(0, N - 1)], recv2.at[pl.ds(0, N - 1)], sems.at[0]).wait()
    pltpu.make_async_copy(send1.at[pl.ds(0, 7)], send1.at[pl.ds(0, 7)], sems.at[2]).wait()


def back(index, upd):
    dt = upd.dtype
    return pl.pallas_call(
        back_kernel,
        out_shape=jax.ShapeDtypeStruct((32, 8192), dt),
        in_specs=[pl.BlockSpec(memory_space=pltpu.SMEM), pl.BlockSpec(memory_space=pltpu.VMEM)],
        out_specs=pl.BlockSpec(memory_space=pltpu.VMEM),
        scratch_shapes=[
            pltpu.VMEM((N, 2, 16, 128), dt),
            pltpu.VMEM((8, 16, 16, 128), dt),
            pltpu.VMEM((8, 16, 16, 128), dt),
            pltpu.SemaphoreType.DMA((4,)),
        ],
        compiler_params=pltpu.CompilerParams(
            collective_id=1, has_side_effects=True, vmem_limit_bytes=40 * 2**20),
        name="back_rows",
    )(index, upd)


def matmul_full(left_arr, right_arr):
    return jnp.dot(left_arr, right_arr, precision=lax.Precision.HIGHEST)


def block_slots(block_owner):
    positions = jnp.arange(block_owner.shape[0], dtype=jnp.int32)
    same_owner = block_owner[:, None] == block_owner[None, :]
    earlier = positions[None, :] < positions[:, None]
    return jnp.sum(jnp.where(same_owner & earlier, 1, 0), axis=1).astype(jnp.int32)


def soap_block(grad_block, left_stat, right_stat, left_rot, right_rot, first_stat, second_stat):
    next_left = 0.95 * left_stat + 0.05 * matmul_full(grad_block, grad_block.T)
    next_right = 0.95 * right_stat + 0.05 * matmul_full(grad_block.T, grad_block)
    rotated = matmul_full(matmul_full(left_rot.T, grad_block), right_rot)
    next_first = 0.9 * first_stat + 0.1 * rotated
    next_second = 0.95 * second_stat + 0.05 * rotated * rotated
    direction = next_first / (1.0 - 0.9**10) / (jnp.sqrt(next_second / (1.0 - 0.95**10)) + 1e-08)
    update = matmul_full(matmul_full(left_rot, direction), right_rot.T).astype(jnp.bfloat16)
    return (next_left, next_right, next_first, next_second, update)


def per_device(grad, block_owner, left_factor, right_factor, left_basis, right_basis, first_moment, second_moment):
    me = lax.axis_index("dp")
    place = 2 * block_owner + block_slots(block_owner)
    hits = place[None, :] == jnp.arange(2 * N, dtype=jnp.int32)[:, None]
    index = jnp.sum(jnp.where(hits, jnp.arange(N, dtype=jnp.int32)[None, :], 0), axis=1)
    filled = jnp.any(hits, axis=1)
    squares = lax.psum(jnp.sum(grad * grad), "dp")
    scale = jnp.minimum(1.0, 0.04 / (jnp.sqrt(squares / (N * grad.size)) + 1e-06))
    blocks = forward(index, grad) * scale
    results = [
        soap_block(blocks[s], left_factor[s], right_factor[s], left_basis[s], right_basis[s], first_moment[s], second_moment[s])
        for s in range(2)
    ]
    mine = lax.dynamic_slice_in_dim(filled, 2 * me, 2, 0)
    olds = (left_factor, right_factor, first_moment, second_moment)
    news = [
        jnp.stack([jnp.where(mine[s], results[s][t], olds[t][s]) for s in range(2)])
        for t in range(4)
    ]
    updates = back(place, jnp.stack([results[s][4] for s in range(2)]))
    return (updates, *news)


def solution(mesh):
    rows, state = P("dp", None), P("dp", None, None)
    return jax.shard_map(
        per_device, mesh=mesh, in_specs=(rows, P()) + (state,) * 6,
        out_specs=(rows,) + (state,) * 4, check_vma=False,
    )
```

```python
import jax
import jax.numpy as jnp
from jax import lax
from jax.experimental import pallas as pl
from jax.experimental.pallas import tpu as pltpu
from jax.sharding import PartitionSpec as P

MESH = pl.DeviceIdType.MESH
N = 128
GROUPS = 8
RANKS = 16
ORDER = 512
STRIDE = 45
UNROLL = 8
LEVELS = 32767.0
FIRST_CORRECTION = 1.0 - 0.9**10
SECOND_CORRECTION = 1.0 - 0.95**10
f32, bf16, i32, i16 = jnp.float32, jnp.bfloat16, jnp.int32, jnp.int16


def split(x):
    high = x.astype(bf16)
    return high, (x - high.astype(f32)).astype(bf16)


def product(left, right, contract):
    def one(a, b):
        return lax.dot_general(a, b, (contract, ((), ())), preferred_element_type=f32)

    (lh, ll), (rh, rl) = left, right
    return one(lh, rh) + one(lh, rl) + one(ll, rh)


def each_peer(me, act):
    def step(_, cur):
        cur = lax.rem(cur + STRIDE, N)
        act(cur)
        return cur

    lax.fori_loop(1, N, step, me, unroll=UNROLL)


def remote(src, dst, send_sem, recv_sem, peer):
    pltpu.make_async_remote_copy(
        src_ref=src, dst_ref=dst, send_sem=send_sem, recv_sem=recv_sem, device_id=(peer,), device_id_type=MESH).start()


def arrive(ref, sem):
    pltpu.make_async_copy(ref, ref, sem).wait()


def step_kernel(
    table, grad, left_basis, right_basis, first, second, left, right,
    updates, new_left, new_right, new_first, new_second,
    grad_v, basis_v, old_v, basis_s, note, notes, send1, recv1, send2, land, grad_s, work_s, back, recv3, send4, recv4,
    loads, sends, recvs,
):
    me = lax.axis_index("dp")
    group, rank = me // RANKS, me % RANKS
    half, part = group // 4, group % 4

    pairs = [(grad, grad_v), (left_basis, basis_v.at[0]), (right_basis, basis_v.at[1]), (first, old_v.at[0]),
             (second, old_v.at[1]), (left, old_v.at[2]), (right, old_v.at[3])]
    copies = [pltpu.make_async_copy(src, dst, loads.at[k]) for k, (src, dst) in enumerate(pairs)]
    for copy in copies:
        copy.start()
    barrier = pltpu.get_barrier_semaphore()
    each_peer(me, lambda peer: pl.semaphore_signal(barrier, inc=1, device_id=(peer,), device_id_type=MESH))

    copies[0].wait()
    values = grad_v[...]
    top = jnp.max(jnp.abs(values), axis=1, keepdims=True)
    squares = jnp.sum(values * values)
    inverse = jnp.where(top > 1e-37, 1.0 / jnp.maximum(top, 1e-37), 0.0)
    row = lax.broadcasted_iota(i32, (32, 128), 0)
    lane = lax.broadcasted_iota(i32, (32, 128), 1)
    tops = jnp.sum(jnp.where(lane == row, top, 0.0), axis=0, keepdims=True)
    note[...] = tops + jnp.where(lane[:1] == 32, squares, 0.0)

    def encode(c, carry):
        for h in range(2):
            for j in range(4):
                col = pl.multiple_of(ORDER * c + 128 * j, 128)
                tile = grad_v[16 * h:16 * h + 16, pl.ds(col, 128)]
                code = (jnp.sqrt(jnp.abs(tile) * inverse[16 * h:16 * h + 16]) * LEVELS + 0.5).astype(i32)
                send1[4 * h + j, c] = jnp.where(tile < 0.0, -code, code).astype(i16)
        return carry

    lax.fori_loop(0, RANKS, encode, 0)
    pl.semaphore_wait(barrier, N - 1)

    for d in range(1, GROUPS):
        to = lax.rem(group + d, GROUPS)
        remote(send1.at[to], recv1.at[group], sends.at[0], recvs.at[0], to * RANKS + rank)
    pltpu.make_async_copy(send1.at[group], recv1.at[group], recvs.at[0]).start()
    each_peer(me, lambda peer: remote(note, notes.at[me], sends.at[1], recvs.at[1], peer))
    pltpu.make_async_copy(note, notes.at[me], recvs.at[1]).start()

    for k in range(2):
        copies[1 + k].wait()
        for s in range(2):
            basis_s[k, s, 0], basis_s[k, s, 1] = split(basis_v[k, s])
    arrive(recv1, recvs.at[0])

    at_row = pl.multiple_of(32 * rank + 16 * half, 16)
    at_col = pl.multiple_of(128 * part, 128)

    def deliver(s, carry):
        place = land.at[s, pl.ds(at_row, 16), pl.ds(at_col, 128)]

        def pack(peer):
            block = table[2 * peer + s]
            send2[s, peer] = recv1[block // RANKS, block % RANKS]

        def post(peer):
            pack(peer)
            remote(send2.at[s, peer], place, sends.at[2], recvs.at[2 + s], peer)

        each_peer(me, post)
        pack(me)
        pltpu.make_async_copy(send2.at[s, me], place, recvs.at[2 + s]).start()
        return carry

    lax.fori_loop(0, 2, deliver, 0)

    arrive(notes, recvs.at[1])
    lanes = lax.broadcasted_iota(i32, (1, 128), 1)
    total = jnp.sum(jnp.where(lanes == 32, jnp.sum(notes[...], axis=0), 0.0), axis=1, keepdims=True)
    scale = jnp.minimum(1.0, 0.04 / (jnp.sqrt(total / (N * 32 * 8192)) + 1e-06))
    for copy in copies[3:]:
        copy.wait()

    def compute(s, carry):
        arrive(land.at[s], recvs.at[2 + s])
        from_group = table[2 * me + s] // RANKS

        def decode(d, inner):
            rows = pl.ds(pl.multiple_of(32 * d, 32), 32)
            tops = notes[from_group * RANKS + d] * scale
            factor = jnp.sum(jnp.where(lane == row, tops, 0.0), axis=1, keepdims=True)
            code = land[s, rows, :].astype(i32).astype(f32) * (1.0 / LEVELS)
            high, low = split(code * jnp.abs(code) * factor)
            grad_s[s, 0, rows, :] = high
            grad_s[s, 1, rows, :] = low
            return inner

        lax.fori_loop(0, RANKS, decode, 0)
        lh, ll, rh, rl = basis_s[0, s, 0], basis_s[0, s, 1], basis_s[1, s, 0], basis_s[1, s, 1]
        half_turned = product((lh, ll), (grad_s[s, 0], grad_s[s, 1]), ((0,), (0,)))
        work_s[0], work_s[1] = split(half_turned)
        turned = product((work_s[0], work_s[1]), (rh, rl), ((1,), (0,)))
        kept = table[2 * N + 2 * me + s] > 0
        moved = jnp.where(kept, 0.9, 1.0) * old_v[0, s] + jnp.where(kept, 0.1, 0.0) * turned
        spread = jnp.where(kept, 0.95, 1.0) * old_v[1, s] + jnp.where(kept, 0.05, 0.0) * turned * turned
        new_first[s] = moved
        new_second[s] = spread
        direction = moved / FIRST_CORRECTION / (jnp.sqrt(spread / SECOND_CORRECTION) + 1e-08)
        work_s[0], work_s[1] = split(direction)
        half_back = product((lh, ll), (work_s[0], work_s[1]), ((1,), (0,)))
        work_s[0], work_s[1] = split(half_back)
        back[s] = product((work_s[0], work_s[1]), (rh, rl), ((1,), (1,))).astype(bf16)

        def place(peer):
            peer_row = pl.multiple_of(32 * (peer % RANKS) + 16 * (peer // 64), 16)
            peer_col = pl.multiple_of(128 * ((peer // RANKS) % 4), 128)
            return back.at[s, pl.ds(peer_row, 16), pl.ds(peer_col, 128)]

        each_peer(me, lambda peer: remote(place(peer), recv3.at[s, me], sends.at[3], recvs.at[4], peer))
        pltpu.make_async_copy(place(me), recv3.at[s, me], recvs.at[4]).start()
        return carry

    lax.fori_loop(0, 2, compute, 0)

    def factors(s, carry):
        kept = table[2 * N + 2 * me + s] > 0
        stay, fresh = jnp.where(kept, 0.95, 1.0), jnp.where(kept, 0.05, 0.0)
        halves = (grad_s[s, 0], grad_s[s, 1])
        new_left[s] = stay * old_v[2, s] + fresh * product(halves, halves, ((1,), (1,)))
        new_right[s] = stay * old_v[3, s] + fresh * product(halves, halves, ((0,), (0,)))
        return carry

    lax.fori_loop(0, 2, factors, 0)

    arrive(recv3, recvs.at[4])

    def collect(g):
        for c in range(RANKS):
            slot = table[4 * N + RANKS * g + c]
            send4[g, c] = recv3[slot % 2, slot // 2]

    for d in range(1, GROUPS):
        to = lax.rem(group + d, GROUPS)
        collect(to)
        remote(send4.at[to], recv4.at[group], sends.at[4], recvs.at[5], to * RANKS + rank)
    collect(group)
    pltpu.make_async_copy(send4.at[group], recv4.at[group], recvs.at[5]).start()
    arrive(recv4, recvs.at[5])

    def unpack(c, carry):
        for h in range(2):
            for j in range(4):
                col = pl.multiple_of(ORDER * c + 128 * j, 128)
                updates[16 * h:16 * h + 16, pl.ds(col, 128)] = recv4[4 * h + j, c]
        return carry

    lax.fori_loop(0, RANKS, unpack, 0)
    others = pl.ds(0, N - 1)
    arrive(send1.at[pl.ds(0, GROUPS - 1)], sends.at[0])
    arrive(notes.at[others], sends.at[1])
    arrive(send4.at[pl.ds(0, GROUPS - 1)], sends.at[4])
    for s in range(2):
        arrive(send2.at[s, others], sends.at[2])
        arrive(recv3.at[s, others], sends.at[3])


def block_slots(block_owner):
    positions = jnp.arange(block_owner.shape[0], dtype=i32)
    same_owner = block_owner[:, None] == block_owner[None, :]
    earlier = positions[None, :] < positions[:, None]
    return jnp.sum(jnp.where(same_owner & earlier, 1, 0), axis=1).astype(i32)


def per_device(grad, block_owner, left_factor, right_factor, left_basis, right_basis, first_moment, second_moment):
    place = 2 * block_owner + block_slots(block_owner)
    hits = place[None, :] == jnp.arange(2 * N, dtype=i32)[:, None]
    index = jnp.sum(jnp.where(hits, jnp.arange(N, dtype=i32)[None, :], 0), axis=1)
    table = jnp.concatenate([index, jnp.any(hits, axis=1).astype(i32), place])
    state = pltpu.VMEM((2, ORDER, ORDER), f32)
    in_hbm = pl.BlockSpec(memory_space=pl.ANY)
    in_vmem = pl.BlockSpec(memory_space=pltpu.VMEM)
    return pl.pallas_call(
        step_kernel,
        out_shape=[pltpu.VMEM(grad.shape, bf16)] + [state] * 4,
        in_specs=[pl.BlockSpec(memory_space=pltpu.SMEM)] + [in_hbm] * 7,
        out_specs=[in_vmem] * 5,
        scratch_shapes=[
            pltpu.VMEM(grad.shape, f32),
            pltpu.VMEM((2, 2, ORDER, ORDER), f32),
            pltpu.VMEM((4, 2, ORDER, ORDER), f32),
            pltpu.VMEM((2, 2, 2, ORDER, ORDER), bf16),
            pltpu.VMEM((1, 128), f32),
            pltpu.VMEM((N, 1, 128), f32),
            pltpu.VMEM((GROUPS, RANKS, 16, 128), i16),
            pltpu.VMEM((GROUPS, RANKS, 16, 128), i16),
            pltpu.VMEM((2, N, 16, 128), i16),
            pltpu.VMEM((2, ORDER, ORDER), i16),
            pltpu.VMEM((2, 2, ORDER, ORDER), bf16),
            pltpu.VMEM((2, ORDER, ORDER), bf16),
            pltpu.VMEM((2, ORDER, ORDER), bf16),
            pltpu.VMEM((2, N, 16, 128), bf16),
            pltpu.VMEM((GROUPS, RANKS, 16, 128), bf16),
            pltpu.VMEM((GROUPS, RANKS, 16, 128), bf16),
            pltpu.SemaphoreType.DMA((7,)),
            pltpu.SemaphoreType.DMA((5,)),
            pltpu.SemaphoreType.DMA((6,)),
        ],
        compiler_params=pltpu.CompilerParams(
            collective_id=0, has_side_effects=True, vmem_limit_bytes=50 * 2**20),
        name="soap_step",
    )(table, grad, left_basis, right_basis, first_moment, second_moment, left_factor, right_factor)


def solution(mesh):
    rows, state = P("dp", None), P("dp", None, None)
    return jax.shard_map(
        per_device, mesh=mesh, in_specs=(rows, P()) + (state,) * 6,
        out_specs=(rows,) + (state,) * 4, check_vma=False,
    )
```

```python
import jax
import jax.numpy as jnp
from jax import lax
from jax.experimental import pallas as pl
from jax.experimental.pallas import tpu as pltpu
from jax.sharding import PartitionSpec as P

MESH = pl.DeviceIdType.MESH
N = 128
GROUPS = 8
RANKS = 16
ORDER = 512
STRIDE = 45
UNROLL = 8
LEVELS = 32767.0
FIRST_CORRECTION = 1.0 - 0.9**10
SECOND_CORRECTION = 1.0 - 0.95**10
f32, bf16, i32, i16 = jnp.float32, jnp.bfloat16, jnp.int32, jnp.int16


def split(x):
    high = x.astype(bf16)
    return high, (x - high.astype(f32)).astype(bf16)


def product(left, right, contract):
    def one(a, b):
        return lax.dot_general(a, b, (contract, ((), ())), preferred_element_type=f32)

    (lh, ll), (rh, rl) = left, right
    return one(lh, rh) + one(lh, rl) + one(ll, rh)


def each_peer(me, act):
    def step(_, cur):
        cur = lax.rem(cur + STRIDE, N)
        act(cur)
        return cur

    lax.fori_loop(1, N, step, me, unroll=UNROLL)


def remote(src, dst, send_sem, recv_sem, peer):
    pltpu.make_async_remote_copy(
        src_ref=src, dst_ref=dst, send_sem=send_sem, recv_sem=recv_sem, device_id=(peer,), device_id_type=MESH).start()


def arrive(ref, sem):
    pltpu.make_async_copy(ref, ref, sem).wait()


def step_kernel(
    owner, grad, left_basis, right_basis, first, second, left, right,
    updates, new_left, new_right, new_first, new_second,
    table_v, table, factor, grad_v, basis_v, old_v, basis_s, note, notes1, notes, send1, recv1, send2, land, grad_s, work_s, back, recv3, send4, recv4,
    loads, sends, recvs,
):
    me = lax.axis_index("dp")
    group, rank = me // RANKS, me % RANKS
    half, part = group // 4, group % 4

    pairs = [(grad, grad_v), (left_basis, basis_v.at[0]), (right_basis, basis_v.at[1]), (first, old_v.at[0]),
             (second, old_v.at[1]), (left, old_v.at[2]), (right, old_v.at[3])]
    copies = [pltpu.make_async_copy(src, dst, loads.at[k]) for k, (src, dst) in enumerate(pairs)]
    for copy in copies:
        copy.start()
    barrier = pltpu.get_barrier_semaphore()
    each_peer(me, lambda peer: pl.semaphore_signal(barrier, inc=1, device_id=(peer,), device_id_type=MESH))

    above = lax.broadcasted_iota(i32, (N, N), 0)
    along = lax.broadcasted_iota(i32, (N, N), 1)
    owners = jnp.broadcast_to(owner[...], (N, N))
    earlier = jnp.where((owners == owners.T) & (above < along), 1, 0)
    places = 2 * owner[...] + jnp.sum(earlier, axis=0, keepdims=True)
    turned_places = jnp.broadcast_to(places, (N, N)).T
    for s in range(2):
        hits = turned_places == 2 * along + s
        table_v[s:s + 1] = jnp.sum(jnp.where(hits, above, 0), axis=0, keepdims=True)
        table_v[2 + s:3 + s] = jnp.sum(jnp.where(hits, 1, 0), axis=0, keepdims=True)
    table_v[4:5] = places
    table_v[5:8] = jnp.zeros((3, N), i32)
    table_copy = pltpu.make_async_copy(table_v, table, loads.at[7])
    table_copy.start()

    copies[0].wait()
    values = grad_v[...]
    top = jnp.max(jnp.abs(values), axis=1, keepdims=True)
    squares = jnp.sum(values * values)
    inverse = jnp.where(top > 1e-37, 1.0 / jnp.maximum(top, 1e-37), 0.0)
    row = lax.broadcasted_iota(i32, (32, 128), 0)
    lane = lax.broadcasted_iota(i32, (32, 128), 1)
    tops = jnp.sum(jnp.where(lane == row, top, 0.0), axis=0, keepdims=True)
    note[...] = tops + jnp.where(lane[:1] == 32, squares, 0.0)

    def encode(c, carry):
        for h in range(2):
            for j in range(4):
                col = pl.multiple_of(ORDER * c + 128 * j, 128)
                tile = grad_v[16 * h:16 * h + 16, pl.ds(col, 128)]
                code = (jnp.sqrt(jnp.abs(tile) * inverse[16 * h:16 * h + 16]) * LEVELS + 0.5).astype(i32)
                send1[4 * h + j, c] = jnp.where(tile < 0.0, -code, code).astype(i16)
        return carry

    lax.fori_loop(0, RANKS, encode, 0)
    pl.semaphore_wait(barrier, N - 1)

    for d in range(1, GROUPS):
        to = lax.rem(group + d, GROUPS)
        remote(note, notes1.at[group], sends.at[1], recvs.at[1], to * RANKS + rank)
        remote(send1.at[to], recv1.at[group], sends.at[0], recvs.at[0], to * RANKS + rank)
    pltpu.make_async_copy(note, notes1.at[group], recvs.at[1]).start()
    pltpu.make_async_copy(send1.at[group], recv1.at[group], recvs.at[0]).start()

    for k in range(2):
        copies[1 + k].wait()
        for s in range(2):
            basis_s[k, s, 0], basis_s[k, s, 1] = split(basis_v[k, s])
    table_copy.wait()
    arrive(notes1, recvs.at[1])
    arrive(recv1, recvs.at[0])

    at_row = pl.multiple_of(32 * rank + 16 * half, 16)
    at_col = pl.multiple_of(128 * part, 128)

    def deliver(s, carry):
        place = land.at[s, pl.ds(at_row, 16), pl.ds(at_col, 128)]

        def pack(peer):
            block = table[s, peer]
            send2[s, peer] = recv1[block // RANKS, block % RANKS]

        def post(peer):
            pack(peer)
            remote(send2.at[s, peer], place, sends.at[2], recvs.at[2 + s], peer)

        each_peer(me, post)
        pack(me)
        pltpu.make_async_copy(send2.at[s, me], place, recvs.at[2 + s]).start()

        @pl.when(s == 0)
        def _():
            for d in range(1, RANKS):
                remote(notes1, notes.at[rank], sends.at[5], recvs.at[6], group * RANKS + lax.rem(rank + d, RANKS))
            pltpu.make_async_copy(notes1, notes.at[rank], recvs.at[6]).start()

        return carry

    lax.fori_loop(0, 2, deliver, 0)

    arrive(notes, recvs.at[6])
    lanes = lax.broadcasted_iota(i32, (1, 128), 1)
    total = jnp.sum(jnp.where(lanes == 32, jnp.sum(notes[...], axis=(0, 1)), 0.0), axis=1, keepdims=True)
    scale = jnp.minimum(1.0, 0.04 / (jnp.sqrt(total / (N * 32 * 8192)) + 1e-06))
    for copy in copies[3:]:
        copy.wait()

    for s in range(2):
        from_group = table[s, me] // RANKS
        for d in range(RANKS):
            tops = notes[d, from_group] * (scale / (LEVELS * LEVELS))
            column = jnp.sum(jnp.where(lane == row, tops, 0.0), axis=1, keepdims=True)
            factor[s, 32 * d:32 * d + 32] = jnp.broadcast_to(column, (32, 128))

    def compute(s, carry):
        arrive(land.at[s], recvs.at[2 + s])

        def decode(d, inner):
            rows = pl.ds(pl.multiple_of(64 * d, 64), 64)
            for j in range(4):
                cols = pl.ds(128 * j, 128)
                code = land[s, rows, cols].astype(i32).astype(f32)
                grad_s[s, 0, rows, cols], grad_s[s, 1, rows, cols] = split(code * jnp.abs(code) * factor[s, rows])
            return inner

        lax.fori_loop(0, ORDER // 64, decode, 0)
        lh, ll, rh, rl = basis_s[0, s, 0], basis_s[0, s, 1], basis_s[1, s, 0], basis_s[1, s, 1]
        half_turned = product((lh, ll), (grad_s[s, 0], grad_s[s, 1]), ((0,), (0,)))
        work_s[0], work_s[1] = split(half_turned)
        turned = product((work_s[0], work_s[1]), (rh, rl), ((1,), (0,)))
        kept = table[2 + s, me] > 0
        moved = jnp.where(kept, 0.9, 1.0) * old_v[0, s] + jnp.where(kept, 0.1, 0.0) * turned
        spread = jnp.where(kept, 0.95, 1.0) * old_v[1, s] + jnp.where(kept, 0.05, 0.0) * turned * turned
        new_first[s] = moved
        new_second[s] = spread
        direction = moved / FIRST_CORRECTION / (jnp.sqrt(spread / SECOND_CORRECTION) + 1e-08)
        work_s[0], work_s[1] = split(direction)
        half_back = product((lh, ll), (work_s[0], work_s[1]), ((1,), (0,)))
        work_s[0], work_s[1] = split(half_back)
        back[s] = product((work_s[0], work_s[1]), (rh, rl), ((1,), (1,))).astype(bf16)

        def place(peer):
            peer_row = pl.multiple_of(32 * (peer % RANKS) + 16 * (peer // 64), 16)
            peer_col = pl.multiple_of(128 * ((peer // RANKS) % 4), 128)
            return back.at[s, pl.ds(peer_row, 16), pl.ds(peer_col, 128)]

        each_peer(me, lambda peer: remote(place(peer), recv3.at[s, me], sends.at[3], recvs.at[4], peer))
        pltpu.make_async_copy(place(me), recv3.at[s, me], recvs.at[4]).start()
        return carry

    lax.fori_loop(0, 2, compute, 0)

    def factors(s, carry):
        kept = table[2 + s, me] > 0
        stay, fresh = jnp.where(kept, 0.95, 1.0), jnp.where(kept, 0.05, 0.0)
        halves = (grad_s[s, 0], grad_s[s, 1])
        new_left[s] = stay * old_v[2, s] + fresh * product(halves, halves, ((1,), (1,)))
        new_right[s] = stay * old_v[3, s] + fresh * product(halves, halves, ((0,), (0,)))
        return carry

    lax.fori_loop(0, 2, factors, 0)

    arrive(recv3, recvs.at[4])

    def collect(g):
        for c in range(RANKS):
            slot = table[4, RANKS * g + c]
            send4[g, c] = recv3[slot % 2, slot // 2]

    for d in range(1, GROUPS):
        to = lax.rem(group + d, GROUPS)
        collect(to)
        remote(send4.at[to], recv4.at[group], sends.at[4], recvs.at[5], to * RANKS + rank)
    collect(group)
    pltpu.make_async_copy(send4.at[group], recv4.at[group], recvs.at[5]).start()
    arrive(recv4, recvs.at[5])

    def unpack(c, carry):
        for h in range(2):
            for j in range(4):
                col = pl.multiple_of(ORDER * c + 128 * j, 128)
                updates[16 * h:16 * h + 16, pl.ds(col, 128)] = recv4[4 * h + j, c]
        return carry

    lax.fori_loop(0, RANKS, unpack, 0)
    others = pl.ds(0, N - 1)
    arrive(send1.at[pl.ds(0, GROUPS - 1)], sends.at[0])
    arrive(notes1.at[pl.ds(0, GROUPS - 1)], sends.at[1])
    arrive(notes.at[pl.ds(0, RANKS - 1)], sends.at[5])
    arrive(send4.at[pl.ds(0, GROUPS - 1)], sends.at[4])
    for s in range(2):
        arrive(send2.at[s, others], sends.at[2])
        arrive(recv3.at[s, others], sends.at[3])


def settle_kernel(*refs):
    count = len(refs) // 2
    copies = [pltpu.make_async_copy(refs[k], refs[count + k], refs[-1].at[k]) for k in range(count)]
    for copy in copies:
        copy.start()
    for copy in copies:
        copy.wait()


def per_device(grad, block_owner, left_factor, right_factor, left_basis, right_basis, first_moment, second_moment):
    state = pltpu.VMEM((2, ORDER, ORDER), f32)
    in_hbm = pl.BlockSpec(memory_space=pl.ANY)
    in_vmem = pl.BlockSpec(memory_space=pltpu.VMEM)
    results = pl.pallas_call(
        step_kernel,
        out_shape=[pltpu.VMEM(grad.shape, bf16)] + [state] * 4,
        in_specs=[in_vmem] + [in_hbm] * 7,
        out_specs=[in_vmem] * 5,
        scratch_shapes=[
            pltpu.VMEM((8, N), i32),
            pltpu.SMEM((8, N), i32),
            pltpu.VMEM((2, ORDER, 128), f32),
            pltpu.VMEM(grad.shape, f32),
            pltpu.VMEM((2, 2, ORDER, ORDER), f32),
            pltpu.VMEM((4, 2, ORDER, ORDER), f32),
            pltpu.VMEM((2, 2, 2, ORDER, ORDER), bf16),
            pltpu.VMEM((1, 128), f32),
            pltpu.VMEM((GROUPS, 1, 128), f32),
            pltpu.VMEM((RANKS, GROUPS, 1, 128), f32),
            pltpu.VMEM((GROUPS, RANKS, 16, 128), i16),
            pltpu.VMEM((GROUPS, RANKS, 16, 128), i16),
            pltpu.VMEM((2, N, 16, 128), i16),
            pltpu.VMEM((2, ORDER, ORDER), i16),
            pltpu.VMEM((2, 2, ORDER, ORDER), bf16),
            pltpu.VMEM((2, ORDER, ORDER), bf16),
            pltpu.VMEM((2, ORDER, ORDER), bf16),
            pltpu.VMEM((2, N, 16, 128), bf16),
            pltpu.VMEM((GROUPS, RANKS, 16, 128), bf16),
            pltpu.VMEM((GROUPS, RANKS, 16, 128), bf16),
            pltpu.SemaphoreType.DMA((8,)),
            pltpu.SemaphoreType.DMA((6,)),
            pltpu.SemaphoreType.DMA((7,)),
        ],
        compiler_params=pltpu.CompilerParams(
            collective_id=0, has_side_effects=True, vmem_limit_bytes=50 * 2**20),
        name="soap_step",
    )(block_owner.reshape(1, N), grad, left_basis, right_basis, first_moment, second_moment, left_factor, right_factor)
    return pl.pallas_call(
        settle_kernel,
        out_shape=[jax.ShapeDtypeStruct(r.shape, r.dtype) for r in results],
        in_specs=[in_hbm] * 5,
        out_specs=[in_hbm] * 5,
        scratch_shapes=[pltpu.SemaphoreType.DMA((5,))],
        compiler_params=pltpu.CompilerParams(vmem_limit_bytes=2**20),
        name="settle",
    )(*results)


def solution(mesh):
    rows, state = P("dp", None), P("dp", None, None)
    return jax.shard_map(
        per_device, mesh=mesh, in_specs=(rows, P()) + (state,) * 6,
        out_specs=(rows,) + (state,) * 4, check_vma=False,
    )
```

```python
import jax
import jax.numpy as jnp
from jax import lax
from jax.experimental import pallas as pl
from jax.experimental.pallas import tpu as pltpu
from jax.sharding import PartitionSpec as P

MESH = pl.DeviceIdType.MESH
N = 128
GROUPS = 8
RANKS = 16
ORDER = 512
STRIDE = 45
UNROLL = 8
LEVELS = 32767.0
FIRST_CORRECTION = 1.0 - 0.9**10
SECOND_CORRECTION = 1.0 - 0.95**10
f32, bf16, i32, i16 = jnp.float32, jnp.bfloat16, jnp.int32, jnp.int16


def split(x):
    high = x.astype(bf16)
    return high, (x - high.astype(f32)).astype(bf16)


def product(left, right, contract):
    def one(a, b):
        return lax.dot_general(a, b, (contract, ((), ())), preferred_element_type=f32)

    (lh, ll), (rh, rl) = left, right
    return one(lh, rh) + one(lh, rl) + one(ll, rh)


def each_peer(me, act):
    def step(_, cur):
        cur = lax.rem(cur + STRIDE, N)
        act(cur)
        return cur

    lax.fori_loop(1, N, step, me, unroll=UNROLL)


def remote(src, dst, send_sem, recv_sem, peer):
    pltpu.make_async_remote_copy(
        src_ref=src, dst_ref=dst, send_sem=send_sem, recv_sem=recv_sem, device_id=(peer,), device_id_type=MESH).start()


def arrive(ref, sem):
    pltpu.make_async_copy(ref, ref, sem).wait()


def step_kernel(
    owner, grad, left_basis, right_basis, first, second, left, right,
    updates, new_left, new_right, new_first, new_second,
    table_v, table, factor, grad_v, basis_v, old_v, basis_s, note, notes1, notes, send1, recv1, send2, land, grad_s, work_s, back, recv3, send4, recv4,
    loads, sends, recvs, arrivals, groups_in,
):
    me = lax.axis_index("dp")
    group, rank = me // RANKS, me % RANKS
    half, part = group // 4, group % 4

    pairs = [(grad, grad_v), (left_basis, basis_v.at[0]), (right_basis, basis_v.at[1]), (first, old_v.at[0]),
             (second, old_v.at[1]), (left, old_v.at[2]), (right, old_v.at[3])]
    copies = [pltpu.make_async_copy(src, dst, loads.at[k]) for k, (src, dst) in enumerate(pairs)]
    copies[0].start()
    barrier = pltpu.get_barrier_semaphore()
    same_rank = [lax.rem(group + d, GROUPS) * RANKS + rank for d in range(1, GROUPS)]
    same_group = [group * RANKS + lax.rem(rank + d, RANKS) for d in range(1, RANKS)]
    for peer in same_rank + same_group:
        pl.semaphore_signal(barrier, inc=1, device_id=(peer,), device_id_type=MESH)

    above = lax.broadcasted_iota(i32, (N, N), 0)
    along = lax.broadcasted_iota(i32, (N, N), 1)
    owners = jnp.broadcast_to(owner[...], (N, N))
    earlier = jnp.where((owners == owners.T) & (above < along), 1, 0)
    places = owner[...] + N * jnp.sum(earlier, axis=0, keepdims=True)
    turned_places = jnp.broadcast_to(places, (N, N)).T
    for s in range(2):
        hits = turned_places == along + N * s
        table_v[s:s + 1] = jnp.sum(jnp.where(hits, above, 0), axis=0, keepdims=True)
        table_v[2 + s:3 + s] = jnp.sum(jnp.where(hits, 1, 0), axis=0, keepdims=True)
    table_v[4:5] = jnp.minimum(places, 2 * N - 1)
    table_v[5:8] = jnp.zeros((3, N), i32)
    table_copy = pltpu.make_async_copy(table_v, table, loads.at[7])
    table_copy.start()

    copies[0].wait()
    for copy in copies[1:]:
        copy.start()
    values = grad_v[...]
    top = jnp.max(jnp.abs(values), axis=1, keepdims=True)
    squares = jnp.sum(values * values)
    inverse = jnp.where(top > 1e-37, 1.0 / jnp.maximum(top, 1e-37), 0.0)
    row = lax.broadcasted_iota(i32, (32, 128), 0)
    lane = lax.broadcasted_iota(i32, (32, 128), 1)
    tops = jnp.sum(jnp.where(lane == row, top, 0.0), axis=0, keepdims=True)
    note[...] = tops + jnp.where(lane[:1] == 32, squares, 0.0)

    def encode(c, carry):
        for h in range(2):
            for j in range(4):
                col = pl.multiple_of(ORDER * c + 128 * j, 128)
                tile = grad_v[16 * h:16 * h + 16, pl.ds(col, 128)]
                code = (jnp.sqrt(jnp.abs(tile) * inverse[16 * h:16 * h + 16]) * LEVELS + 0.5).astype(i32)
                send1[4 * h + j, c] = jnp.where(tile < 0.0, -code, code).astype(i16)
        return carry

    lax.fori_loop(0, RANKS, encode, 0)
    pl.semaphore_wait(barrier, len(same_rank) + len(same_group))
    for peer in same_rank:
        pl.semaphore_signal(groups_in, inc=1, device_id=(peer,), device_id_type=MESH)

    own_blocks = pl.ds(group * RANKS, RANKS)
    for d in range(1, GROUPS):
        to = lax.rem(group + d, GROUPS)
        remote(note, notes1.at[group], sends.at[1], recvs.at[1], to * RANKS + rank)
        remote(send1.at[to], recv1.at[own_blocks], sends.at[0], recvs.at[0], to * RANKS + rank)
    pltpu.make_async_copy(note, notes1.at[group], recvs.at[1]).start()
    pltpu.make_async_copy(send1.at[group], recv1.at[own_blocks], recvs.at[0]).start()

    for k in range(2):
        copies[1 + k].wait()
        for s in range(2):
            basis_s[k, s, 0], basis_s[k, s, 1] = split(basis_v[k, s])
    table_copy.wait()
    pl.semaphore_wait(groups_in, len(same_rank))
    arrive(notes1, recvs.at[1])
    arrive(recv1, recvs.at[0])

    at_row = pl.multiple_of(32 * rank + 16 * half, 16)
    at_col = pl.multiple_of(128 * part, 128)

    def deliver(s, carry):
        place = land.at[s, pl.ds(at_row, 16), pl.ds(at_col, 128)]

        def pack(peer):
            send2[s, peer] = recv1[table[s, peer]]

        def post(peer):
            pack(peer)
            remote(send2.at[s, peer], place, sends.at[2], recvs.at[2 + s], peer)

        each_peer(me, post)
        pack(me)
        pltpu.make_async_copy(send2.at[s, me], place, recvs.at[2 + s]).start()

        @pl.when(s == 0)
        def _():
            for d in range(1, RANKS):
                remote(notes1, notes.at[rank], sends.at[5], recvs.at[6], group * RANKS + lax.rem(rank + d, RANKS))
            pltpu.make_async_copy(notes1, notes.at[rank], recvs.at[6]).start()

        return carry

    lax.fori_loop(0, 2, deliver, 0)

    arrive(notes, recvs.at[6])
    lanes = lax.broadcasted_iota(i32, (1, 128), 1)
    total = jnp.sum(jnp.where(lanes == 32, jnp.sum(notes[...], axis=(0, 1)), 0.0), axis=1, keepdims=True)
    scale = jnp.minimum(1.0, 0.04 / (jnp.sqrt(total / (N * 32 * 8192)) + 1e-06))
    for copy in copies[3:]:
        copy.wait()

    for s in range(2):
        from_group = table[s, me] // RANKS
        for d in range(RANKS):
            tops = notes[d, from_group] * (scale / (LEVELS * LEVELS))
            column = jnp.sum(jnp.where(lane == row, tops, 0.0), axis=1, keepdims=True)
            factor[s, 32 * d:32 * d + 32] = jnp.broadcast_to(column, (32, 128))

    def compute(s, carry):
        arrive(land.at[s], recvs.at[2 + s])

        def decode(d, inner):
            rows = pl.ds(pl.multiple_of(64 * d, 64), 64)
            for j in range(4):
                cols = pl.ds(128 * j, 128)
                code = land[s, rows, cols].astype(i32).astype(f32)
                grad_s[s, 0, rows, cols], grad_s[s, 1, rows, cols] = split(code * jnp.abs(code) * factor[s, rows])
            return inner

        lax.fori_loop(0, ORDER // 64, decode, 0)
        lh, ll, rh, rl = basis_s[0, s, 0], basis_s[0, s, 1], basis_s[1, s, 0], basis_s[1, s, 1]
        half_turned = product((lh, ll), (grad_s[s, 0], grad_s[s, 1]), ((0,), (0,)))
        work_s[0], work_s[1] = split(half_turned)
        turned = product((work_s[0], work_s[1]), (rh, rl), ((1,), (0,)))
        kept = table[2 + s, me] > 0
        moved = jnp.where(kept, 0.9, 1.0) * old_v[0, s] + jnp.where(kept, 0.1, 0.0) * turned
        spread = jnp.where(kept, 0.95, 1.0) * old_v[1, s] + jnp.where(kept, 0.05, 0.0) * turned * turned
        new_first[s] = moved
        new_second[s] = spread
        direction = moved / FIRST_CORRECTION / (jnp.sqrt(spread / SECOND_CORRECTION) + 1e-08)
        work_s[0], work_s[1] = split(direction)
        half_back = product((lh, ll), (work_s[0], work_s[1]), ((1,), (0,)))
        work_s[0], work_s[1] = split(half_back)
        update = product((work_s[0], work_s[1]), (rh, rl), ((1,), (1,))).astype(bf16)
        for i in range(N):
            top_row, left_col = 32 * (i % RANKS) + 16 * (i // 64), 128 * (i // RANKS % 4)
            back[s, i] = update[top_row:top_row + 16, left_col:left_col + 128]
        mine = recv3.at[s * N + me]
        each_peer(me, lambda peer: remote(back.at[s, peer], mine, sends.at[3], recvs.at[4], peer))
        pltpu.make_async_copy(back.at[s, me], mine, recvs.at[4]).start()
        return carry

    lax.fori_loop(0, 2, compute, 0)

    def factors(s, carry):
        kept = table[2 + s, me] > 0
        stay, fresh = jnp.where(kept, 0.95, 1.0), jnp.where(kept, 0.05, 0.0)
        halves = (grad_s[s, 0], grad_s[s, 1])
        new_left[s] = stay * old_v[2, s] + fresh * product(halves, halves, ((1,), (1,)))
        new_right[s] = stay * old_v[3, s] + fresh * product(halves, halves, ((0,), (0,)))
        return carry

    lax.fori_loop(0, 2, factors, 0)

    arrive(recv3, recvs.at[4])

    def collect(g):
        for c in range(RANKS):
            send4[g, c] = recv3[table[4, RANKS * g + c]]

    for d in range(1, GROUPS):
        to = lax.rem(group + d, GROUPS)
        collect(to)
        remote(send4.at[to], recv4.at[group], sends.at[4], arrivals.at[d], to * RANKS + rank)
    collect(group)
    pltpu.make_async_copy(send4.at[group], recv4.at[group], arrivals.at[0]).start()
    for d in range(GROUPS):
        source = lax.rem(group + GROUPS - d, GROUPS)
        arrive(recv4.at[source], arrivals.at[d])
        source_row = pl.multiple_of(16 * (source // 4), 16)
        source_col = 128 * lax.rem(source, 4)
        for c in range(RANKS):
            col = pl.multiple_of(ORDER * c + source_col, 128)
            updates[pl.ds(source_row, 16), pl.ds(col, 128)] = recv4[source, c]
    others = pl.ds(0, N - 1)
    arrive(send1.at[pl.ds(0, GROUPS - 1)], sends.at[0])
    arrive(notes1.at[pl.ds(0, GROUPS - 1)], sends.at[1])
    arrive(notes.at[pl.ds(0, RANKS - 1)], sends.at[5])
    arrive(send4.at[pl.ds(0, GROUPS - 1)], sends.at[4])
    for s in range(2):
        arrive(send2.at[s, others], sends.at[2])
        arrive(recv3.at[others], sends.at[3])


def settle_kernel(*refs):
    count = len(refs) // 2
    copies = [pltpu.make_async_copy(refs[k], refs[count + k], refs[-1].at[k]) for k in range(count)]
    for copy in copies:
        copy.start()
    for copy in copies:
        copy.wait()


def per_device(grad, block_owner, left_factor, right_factor, left_basis, right_basis, first_moment, second_moment):
    state = pltpu.VMEM((2, ORDER, ORDER), f32)
    in_hbm = pl.BlockSpec(memory_space=pl.ANY)
    in_vmem = pl.BlockSpec(memory_space=pltpu.VMEM)
    results = pl.pallas_call(
        step_kernel,
        out_shape=[pltpu.VMEM(grad.shape, bf16)] + [state] * 4,
        in_specs=[in_vmem] + [in_hbm] * 7,
        out_specs=[in_vmem] * 5,
        scratch_shapes=[
            pltpu.VMEM((8, N), i32),
            pltpu.SMEM((8, N), i32),
            pltpu.VMEM((2, ORDER, 128), f32),
            pltpu.VMEM(grad.shape, f32),
            pltpu.VMEM((2, 2, ORDER, ORDER), f32),
            pltpu.VMEM((4, 2, ORDER, ORDER), f32),
            pltpu.VMEM((2, 2, 2, ORDER, ORDER), bf16),
            pltpu.VMEM((1, 128), f32),
            pltpu.VMEM((GROUPS, 1, 128), f32),
            pltpu.VMEM((RANKS, GROUPS, 1, 128), f32),
            pltpu.VMEM((GROUPS, RANKS, 16, 128), i16),
            pltpu.VMEM((N, 16, 128), i16),
            pltpu.VMEM((2, N, 16, 128), i16),
            pltpu.VMEM((2, ORDER, ORDER), i16),
            pltpu.VMEM((2, 2, ORDER, ORDER), bf16),
            pltpu.VMEM((2, ORDER, ORDER), bf16),
            pltpu.VMEM((2, N, 16, 128), bf16),
            pltpu.VMEM((2 * N, 16, 128), bf16),
            pltpu.VMEM((GROUPS, RANKS, 16, 128), bf16),
            pltpu.VMEM((GROUPS, RANKS, 16, 128), bf16),
            pltpu.SemaphoreType.DMA((8,)),
            pltpu.SemaphoreType.DMA((6,)),
            pltpu.SemaphoreType.DMA((7,)),
            pltpu.SemaphoreType.DMA((GROUPS,)),
            pltpu.SemaphoreType.REGULAR,
        ],
        compiler_params=pltpu.CompilerParams(
            collective_id=0, has_side_effects=True, vmem_limit_bytes=50 * 2**20),
        name="soap_step",
    )(block_owner.reshape(1, N), grad, left_basis, right_basis, first_moment, second_moment, left_factor, right_factor)
    return pl.pallas_call(
        settle_kernel,
        out_shape=[jax.ShapeDtypeStruct(r.shape, r.dtype) for r in results],
        in_specs=[in_hbm] * 5,
        out_specs=[in_hbm] * 5,
        scratch_shapes=[pltpu.SemaphoreType.DMA((5,))],
        compiler_params=pltpu.CompilerParams(vmem_limit_bytes=2**20),
        name="settle",
    )(*results)


def solution(mesh):
    rows, state = P("dp", None), P("dp", None, None)
    return jax.shard_map(
        per_device, mesh=mesh, in_specs=(rows, P()) + (state,) * 6,
        out_specs=(rows,) + (state,) * 4, check_vma=False,
    )
```

```python
import jax
import jax.numpy as jnp
from jax import lax
from jax.experimental import pallas as pl
from jax.experimental.pallas import tpu as pltpu
from jax.sharding import PartitionSpec as P

MESH = pl.DeviceIdType.MESH
N = 128
GROUPS = 8
RANKS = 16
ORDER = 512
STRIDE = 45
UNROLL = 16
LEVELS = 32767.0
FIRST_CORRECTION = 1.0 - 0.9**10
SECOND_CORRECTION = 1.0 - 0.95**10
f32, bf16, i32, i16 = jnp.float32, jnp.bfloat16, jnp.int32, jnp.int16


def split(x):
    high = x.astype(bf16)
    return high, (x - high.astype(f32)).astype(bf16)


def product(left, right, contract):
    def one(a, b):
        return lax.dot_general(a, b, (contract, ((), ())), preferred_element_type=f32)

    (lh, ll), (rh, rl) = left, right
    return one(lh, rh) + one(lh, rl) + one(ll, rh)


def each_peer(me, act):
    def step(_, cur):
        cur = lax.rem(cur + STRIDE, N)
        act(cur)
        return cur

    lax.fori_loop(1, N, step, me, unroll=UNROLL)


def remote(src, dst, send_sem, recv_sem, peer):
    pltpu.make_async_remote_copy(
        src_ref=src, dst_ref=dst, send_sem=send_sem, recv_sem=recv_sem, device_id=(peer,), device_id_type=MESH).start()


def arrive(ref, sem):
    pltpu.make_async_copy(ref, ref, sem).wait()


def step_kernel(
    owner, grad, left_basis, right_basis, first, second, left, right,
    updates, new_left, new_right, new_first, new_second,
    table_v, table, factor, grad_v, basis_v, old_v, basis_s, note, notes1, notes, inverse_v, send1, recv1, send2, land, grad_s, work_s, back, recv3, send4, recv4,
    loads, sends, recvs, arrivals, groups_in,
):
    me = lax.axis_index("dp")
    group, rank = me // RANKS, me % RANKS
    half, part = group // 4, group % 4

    pairs = [(grad, grad_v), (left_basis, basis_v.at[0]), (right_basis, basis_v.at[1]), (first, old_v.at[0]),
             (second, old_v.at[1]), (left, old_v.at[2]), (right, old_v.at[3])]
    copies = [pltpu.make_async_copy(src, dst, loads.at[k]) for k, (src, dst) in enumerate(pairs)]
    copies[0].start()
    barrier = pltpu.get_barrier_semaphore()
    same_rank = [lax.rem(group + d, GROUPS) * RANKS + rank for d in range(1, GROUPS)]
    same_group = [group * RANKS + lax.rem(rank + d, RANKS) for d in range(1, RANKS)]
    for peer in same_rank + same_group:
        pl.semaphore_signal(barrier, inc=1, device_id=(peer,), device_id_type=MESH)

    copies[0].wait()
    values = grad_v[...]
    top = jnp.max(jnp.abs(values), axis=1, keepdims=True)
    squares = jnp.sum(values * values)
    inverse = jnp.where(top > 1e-37, 1.0 / jnp.maximum(top, 1e-37), 0.0)
    row = lax.broadcasted_iota(i32, (32, 128), 0)
    lane = lax.broadcasted_iota(i32, (32, 128), 1)
    tops = jnp.sum(jnp.where(lane == row, top, 0.0), axis=0, keepdims=True)
    note[...] = tops + jnp.where(lane[:1] == 32, squares, 0.0)

    def encode(to):
        rows = pl.ds(pl.multiple_of(16 * (to // 4), 16), 16)
        scales = inverse_v[rows]
        for c in range(RANKS):
            tile = grad_v[rows, pl.ds(pl.multiple_of(ORDER * c + 128 * (to % 4), 128), 128)]
            code = (jnp.sqrt(jnp.abs(tile) * scales) * LEVELS + 0.5).astype(i32)
            send1[to, c] = jnp.where(tile < 0.0, -code, code).astype(i16)

    inverse_v[...] = jnp.broadcast_to(inverse, (32, 128))
    own_blocks = pl.ds(group * RANKS, RANKS)
    pl.semaphore_wait(barrier, len(same_rank) + len(same_group))

    def spread(d, carry):
        to = lax.rem(group + d, GROUPS)
        peer = to * RANKS + rank
        encode(to)
        remote(send1.at[to], recv1.at[own_blocks], sends.at[0], recvs.at[0], peer)
        remote(note, notes1.at[group], sends.at[1], recvs.at[1], peer)
        pl.semaphore_signal(groups_in, inc=1, device_id=(peer,), device_id_type=MESH)
        return carry

    lax.fori_loop(1, GROUPS, spread, 0)
    for copy in copies[1:]:
        copy.start()
    encode(group)
    pltpu.make_async_copy(send1.at[group], recv1.at[own_blocks], recvs.at[0]).start()
    pltpu.make_async_copy(note, notes1.at[group], recvs.at[1]).start()

    above = lax.broadcasted_iota(i32, (N, N), 0)
    along = lax.broadcasted_iota(i32, (N, N), 1)
    owners = jnp.broadcast_to(owner[...], (N, N))
    earlier = jnp.where((owners == owners.T) & (above < along), 1, 0)
    places = owner[...] + N * jnp.sum(earlier, axis=0, keepdims=True)
    turned_places = jnp.broadcast_to(places, (N, N)).T
    for s in range(2):
        hits = turned_places == along + N * s
        table_v[s:s + 1] = jnp.sum(jnp.where(hits, above, 0), axis=0, keepdims=True)
        table_v[2 + s:3 + s] = jnp.sum(jnp.where(hits, 1, 0), axis=0, keepdims=True)
    table_v[4:5] = jnp.minimum(places, 2 * N - 1)
    table_v[5:8] = jnp.zeros((3, N), i32)
    table_copy = pltpu.make_async_copy(table_v, table, loads.at[7])
    table_copy.start()

    for k in range(2):
        copies[1 + k].wait()
        for s in range(2):
            basis_s[k, s, 0], basis_s[k, s, 1] = split(basis_v[k, s])
    table_copy.wait()
    pl.semaphore_wait(groups_in, len(same_rank))
    arrive(notes1, recvs.at[1])
    arrive(recv1, recvs.at[0])

    at_row = pl.multiple_of(32 * rank + 16 * half, 16)
    at_col = pl.multiple_of(128 * part, 128)

    def deliver(s, carry):
        place = land.at[s, pl.ds(at_row, 16), pl.ds(at_col, 128)]

        def pack(peer):
            send2[s, peer] = recv1[table[s, peer]]

        def post(peer):
            pack(peer)
            remote(send2.at[s, peer], place, sends.at[2], recvs.at[2 + s], peer)

        each_peer(me, post)
        pack(me)
        pltpu.make_async_copy(send2.at[s, me], place, recvs.at[2 + s]).start()

        @pl.when(s == 0)
        def _():
            for d in range(1, RANKS):
                remote(notes1, notes.at[rank], sends.at[5], recvs.at[6], group * RANKS + lax.rem(rank + d, RANKS))
            pltpu.make_async_copy(notes1, notes.at[rank], recvs.at[6]).start()

        return carry

    lax.fori_loop(0, 2, deliver, 0)

    arrive(notes, recvs.at[6])
    lanes = lax.broadcasted_iota(i32, (1, 128), 1)
    total = jnp.sum(jnp.where(lanes == 32, jnp.sum(notes[...], axis=(0, 1)), 0.0), axis=1, keepdims=True)
    scale = jnp.minimum(1.0, 0.04 / (jnp.sqrt(total / (N * 32 * 8192)) + 1e-06))
    for copy in copies[3:]:
        copy.wait()

    for s in range(2):
        from_group = table[s, me] // RANKS
        for d in range(RANKS):
            tops = notes[d, from_group] * (scale / (LEVELS * LEVELS))
            column = jnp.sum(jnp.where(lane == row, tops, 0.0), axis=1, keepdims=True)
            factor[s, 32 * d:32 * d + 32] = jnp.broadcast_to(column, (32, 128))

    def compute(s, carry):
        arrive(land.at[s], recvs.at[2 + s])

        def decode(d, inner):
            rows = pl.ds(pl.multiple_of(64 * d, 64), 64)
            for j in range(4):
                cols = pl.ds(128 * j, 128)
                code = land[s, rows, cols].astype(i32).astype(f32)
                grad_s[s, 0, rows, cols], grad_s[s, 1, rows, cols] = split(code * jnp.abs(code) * factor[s, rows])
            return inner

        lax.fori_loop(0, ORDER // 64, decode, 0)
        lh, ll, rh, rl = basis_s[0, s, 0], basis_s[0, s, 1], basis_s[1, s, 0], basis_s[1, s, 1]
        half_turned = product((lh, ll), (grad_s[s, 0], grad_s[s, 1]), ((0,), (0,)))
        work_s[0], work_s[1] = split(half_turned)
        turned = product((work_s[0], work_s[1]), (rh, rl), ((1,), (0,)))
        kept = table[2 + s, me] > 0
        moved = jnp.where(kept, 0.9, 1.0) * old_v[0, s] + jnp.where(kept, 0.1, 0.0) * turned
        spread = jnp.where(kept, 0.95, 1.0) * old_v[1, s] + jnp.where(kept, 0.05, 0.0) * turned * turned
        new_first[s] = moved
        new_second[s] = spread
        direction = moved * (1.0 / FIRST_CORRECTION) / (jnp.sqrt(spread * (1.0 / SECOND_CORRECTION)) + 1e-08)
        work_s[0], work_s[1] = split(direction)
        half_back = product((lh, ll), (work_s[0], work_s[1]), ((1,), (0,)))
        work_s[0], work_s[1] = split(half_back)
        update = product((work_s[0], work_s[1]), (rh, rl), ((1,), (1,))).astype(bf16)
        for i in range(N):
            top_row, left_col = 32 * (i % RANKS) + 16 * (i // 64), 128 * (i // RANKS % 4)
            back[s, i] = update[top_row:top_row + 16, left_col:left_col + 128]
        mine = recv3.at[s * N + me]
        each_peer(me, lambda peer: remote(back.at[s, peer], mine, sends.at[3], recvs.at[4], peer))
        pltpu.make_async_copy(back.at[s, me], mine, recvs.at[4]).start()
        return carry

    lax.fori_loop(0, 2, compute, 0)

    def factors(s, carry):
        kept = table[2 + s, me] > 0
        stay, fresh = jnp.where(kept, 0.95, 1.0), jnp.where(kept, 0.05, 0.0)
        halves = (grad_s[s, 0], grad_s[s, 1])
        new_left[s] = stay * old_v[2, s] + fresh * product(halves, halves, ((1,), (1,)))
        new_right[s] = stay * old_v[3, s] + fresh * product(halves, halves, ((0,), (0,)))
        return carry

    lax.fori_loop(0, 2, factors, 0)

    arrive(recv3, recvs.at[4])

    def collect(g):
        for c in range(RANKS):
            send4[g, c] = recv3[table[4, RANKS * g + c]]

    for d in range(1, GROUPS):
        to = lax.rem(group + d, GROUPS)
        collect(to)
        remote(send4.at[to], recv4.at[group], sends.at[4], arrivals.at[d], to * RANKS + rank)
    collect(group)
    pltpu.make_async_copy(send4.at[group], recv4.at[group], arrivals.at[0]).start()
    for d in range(GROUPS):
        source = lax.rem(group + GROUPS - d, GROUPS)
        arrive(recv4.at[source], arrivals.at[d])
        source_row = pl.multiple_of(16 * (source // 4), 16)
        source_col = 128 * lax.rem(source, 4)
        for c in range(RANKS):
            col = pl.multiple_of(ORDER * c + source_col, 128)
            updates[pl.ds(source_row, 16), pl.ds(col, 128)] = recv4[source, c]
    others = pl.ds(0, N - 1)
    arrive(send1.at[pl.ds(0, GROUPS - 1)], sends.at[0])
    arrive(notes1.at[pl.ds(0, GROUPS - 1)], sends.at[1])
    arrive(notes.at[pl.ds(0, RANKS - 1)], sends.at[5])
    arrive(send4.at[pl.ds(0, GROUPS - 1)], sends.at[4])
    for s in range(2):
        arrive(send2.at[s, others], sends.at[2])
        arrive(recv3.at[others], sends.at[3])


def settle_kernel(*refs):
    count = len(refs) // 2
    copies = [pltpu.make_async_copy(refs[k], refs[count + k], refs[-1].at[k]) for k in range(count)]
    for copy in copies:
        copy.start()
    for copy in copies:
        copy.wait()


def per_device(grad, block_owner, left_factor, right_factor, left_basis, right_basis, first_moment, second_moment):
    state = pltpu.VMEM((2, ORDER, ORDER), f32)
    in_hbm = pl.BlockSpec(memory_space=pl.ANY)
    in_vmem = pl.BlockSpec(memory_space=pltpu.VMEM)
    results = pl.pallas_call(
        step_kernel,
        out_shape=[pltpu.VMEM(grad.shape, bf16)] + [state] * 4,
        in_specs=[in_vmem] + [in_hbm] * 7,
        out_specs=[in_vmem] * 5,
        scratch_shapes=[
            pltpu.VMEM((8, N), i32),
            pltpu.SMEM((8, N), i32),
            pltpu.VMEM((2, ORDER, 128), f32),
            pltpu.VMEM(grad.shape, f32),
            pltpu.VMEM((2, 2, ORDER, ORDER), f32),
            pltpu.VMEM((4, 2, ORDER, ORDER), f32),
            pltpu.VMEM((2, 2, 2, ORDER, ORDER), bf16),
            pltpu.VMEM((1, 128), f32),
            pltpu.VMEM((GROUPS, 1, 128), f32),
            pltpu.VMEM((RANKS, GROUPS, 1, 128), f32),
            pltpu.VMEM((32, 128), f32),
            pltpu.VMEM((GROUPS, RANKS, 16, 128), i16),
            pltpu.VMEM((N, 16, 128), i16),
            pltpu.VMEM((2, N, 16, 128), i16),
            pltpu.VMEM((2, ORDER, ORDER), i16),
            pltpu.VMEM((2, 2, ORDER, ORDER), bf16),
            pltpu.VMEM((2, ORDER, ORDER), bf16),
            pltpu.VMEM((2, N, 16, 128), bf16),
            pltpu.VMEM((2 * N, 16, 128), bf16),
            pltpu.VMEM((GROUPS, RANKS, 16, 128), bf16),
            pltpu.VMEM((GROUPS, RANKS, 16, 128), bf16),
            pltpu.SemaphoreType.DMA((8,)),
            pltpu.SemaphoreType.DMA((6,)),
            pltpu.SemaphoreType.DMA((7,)),
            pltpu.SemaphoreType.DMA((GROUPS,)),
            pltpu.SemaphoreType.REGULAR,
        ],
        compiler_params=pltpu.CompilerParams(
            collective_id=0, has_side_effects=True, vmem_limit_bytes=50 * 2**20),
        name="soap_step",
    )(block_owner.reshape(1, N), grad, left_basis, right_basis, first_moment, second_moment, left_factor, right_factor)
    return pl.pallas_call(
        settle_kernel,
        out_shape=[jax.ShapeDtypeStruct(r.shape, r.dtype) for r in results],
        in_specs=[in_hbm] * 5,
        out_specs=[in_hbm] * 5,
        scratch_shapes=[pltpu.SemaphoreType.DMA((5,))],
        compiler_params=pltpu.CompilerParams(vmem_limit_bytes=2**20),
        name="settle",
    )(*results)


def solution(mesh):
    rows, state = P("dp", None), P("dp", None, None)
    return jax.shard_map(
        per_device, mesh=mesh, in_specs=(rows, P()) + (state,) * 6,
        out_specs=(rows,) + (state,) * 4, check_vma=False,
    )
```

```python
import jax
import jax.numpy as jnp
from jax import lax
from jax.experimental import pallas as pl
from jax.experimental.pallas import tpu as pltpu
from jax.sharding import PartitionSpec as P

MESH = pl.DeviceIdType.MESH
N = 128
GROUPS = 8
RANKS = 16
ORDER = 512
STRIDE = 45
UNROLL = 16
LEVELS = 32767.0
FIRST_CORRECTION = 1.0 - 0.9**10
SECOND_CORRECTION = 1.0 - 0.95**10
f32, bf16, i32, i16 = jnp.float32, jnp.bfloat16, jnp.int32, jnp.int16


def split(x):
    high = x.astype(bf16)
    return high, (x - high.astype(f32)).astype(bf16)


def product(left, right, contract):
    def one(a, b):
        return lax.dot_general(a, b, (contract, ((), ())), preferred_element_type=f32)

    (lh, ll), (rh, rl) = left, right
    return one(lh, rh) + one(lh, rl) + one(ll, rh)


def each_peer(me, act):
    def step(_, cur):
        cur = lax.rem(cur + STRIDE, N)
        act(cur)
        return cur

    lax.fori_loop(1, N, step, me, unroll=UNROLL)


def remote(src, dst, send_sem, recv_sem, peer):
    pltpu.make_async_remote_copy(
        src_ref=src, dst_ref=dst, send_sem=send_sem, recv_sem=recv_sem, device_id=(peer,), device_id_type=MESH).start()


def arrive(ref, sem):
    pltpu.make_async_copy(ref, ref, sem).wait()


def step_kernel(
    owner, grad, left_basis, right_basis, first, second, left, right,
    updates, new_left, new_right, new_first, new_second,
    table_v, table, factor, grad_v, basis_v, old_v, basis_s, turned_s, note, notes1, notes, inverse_v, send1, recv1, send2, land, grad_s, work_s, back, recv3, send4, recv4,
    loads, sends, recvs, arrivals, groups_in,
):
    me = lax.axis_index("dp")
    group, rank = me // RANKS, me % RANKS
    half, part = group // 4, group % 4

    pairs = [(grad, grad_v), (left_basis, basis_v.at[0]), (right_basis, basis_v.at[1]), (first, old_v.at[0]),
             (second, old_v.at[1]), (left, old_v.at[2]), (right, old_v.at[3])]
    copies = [pltpu.make_async_copy(src, dst, loads.at[k]) for k, (src, dst) in enumerate(pairs)]
    copies[0].start()
    barrier = pltpu.get_barrier_semaphore()
    same_rank = [lax.rem(group + d, GROUPS) * RANKS + rank for d in range(1, GROUPS)]
    same_group = [group * RANKS + lax.rem(rank + d, RANKS) for d in range(1, RANKS)]
    for peer in same_rank + same_group:
        pl.semaphore_signal(barrier, inc=1, device_id=(peer,), device_id_type=MESH)

    copies[0].wait()
    values = grad_v[...]
    top = jnp.max(jnp.abs(values), axis=1, keepdims=True)
    squares = jnp.sum(values * values)
    inverse = jnp.where(top > 1e-37, 1.0 / jnp.maximum(top, 1e-37), 0.0)
    row = lax.broadcasted_iota(i32, (32, 128), 0)
    lane = lax.broadcasted_iota(i32, (32, 128), 1)
    tops = jnp.sum(jnp.where(lane == row, top, 0.0), axis=0, keepdims=True)
    note[...] = tops + jnp.where(lane[:1] == 32, squares, 0.0)

    def encode(to):
        rows = pl.ds(pl.multiple_of(16 * (to // 4), 16), 16)
        scales = inverse_v[rows]
        for c in range(RANKS):
            tile = grad_v[rows, pl.ds(pl.multiple_of(ORDER * c + 128 * (to % 4), 128), 128)]
            code = (jnp.sqrt(jnp.abs(tile) * scales) * LEVELS + 0.5).astype(i32)
            send1[to, c] = jnp.where(tile < 0.0, -code, code).astype(i16)

    inverse_v[...] = jnp.broadcast_to(inverse, (32, 128))
    own_blocks = pl.ds(group * RANKS, RANKS)
    pl.semaphore_wait(barrier, len(same_rank) + len(same_group))

    def spread(d, carry):
        to = lax.rem(group + d, GROUPS)
        peer = to * RANKS + rank
        encode(to)
        remote(send1.at[to], recv1.at[own_blocks], sends.at[0], recvs.at[0], peer)
        remote(note, notes1.at[group], sends.at[1], recvs.at[1], peer)
        pl.semaphore_signal(groups_in, inc=1, device_id=(peer,), device_id_type=MESH)
        return carry

    lax.fori_loop(1, GROUPS, spread, 0)
    for copy in copies[1:]:
        copy.start()
    encode(group)
    pltpu.make_async_copy(send1.at[group], recv1.at[own_blocks], recvs.at[0]).start()
    pltpu.make_async_copy(note, notes1.at[group], recvs.at[1]).start()

    above = lax.broadcasted_iota(i32, (N, N), 0)
    along = lax.broadcasted_iota(i32, (N, N), 1)
    owners = jnp.broadcast_to(owner[...], (N, N))
    earlier = jnp.where((owners == owners.T) & (above < along), 1, 0)
    places = owner[...] + N * jnp.sum(earlier, axis=0, keepdims=True)
    turned_places = jnp.broadcast_to(places, (N, N)).T
    for s in range(2):
        hits = turned_places == along + N * s
        table_v[s:s + 1] = jnp.sum(jnp.where(hits, above, 0), axis=0, keepdims=True)
        table_v[2 + s:3 + s] = jnp.sum(jnp.where(hits, 1, 0), axis=0, keepdims=True)
    table_v[4:5] = jnp.minimum(places, 2 * N - 1)
    table_v[5:8] = jnp.zeros((3, N), i32)
    table_copy = pltpu.make_async_copy(table_v, table, loads.at[7])
    table_copy.start()

    for k in range(2):
        copies[1 + k].wait()
        for s in range(2):
            basis_s[k, s, 0], basis_s[k, s, 1] = split(basis_v[k, s])
            turned_s[k, s, 0], turned_s[k, s, 1] = split(basis_v[k, s].T)
    table_copy.wait()
    pl.semaphore_wait(groups_in, len(same_rank))
    arrive(notes1, recvs.at[1])
    arrive(recv1, recvs.at[0])

    at_row = pl.multiple_of(32 * rank + 16 * half, 16)
    at_col = pl.multiple_of(128 * part, 128)

    def deliver(s, carry):
        place = land.at[s, pl.ds(at_row, 16), pl.ds(at_col, 128)]

        def pack(peer):
            send2[s, peer] = recv1[table[s, peer]]

        def post(peer):
            pack(peer)
            remote(send2.at[s, peer], place, sends.at[2], recvs.at[2 + s], peer)

        each_peer(me, post)
        pack(me)
        pltpu.make_async_copy(send2.at[s, me], place, recvs.at[2 + s]).start()

        @pl.when(s == 0)
        def _():
            for d in range(1, RANKS):
                remote(notes1, notes.at[rank], sends.at[5], recvs.at[6], group * RANKS + lax.rem(rank + d, RANKS))
            pltpu.make_async_copy(notes1, notes.at[rank], recvs.at[6]).start()

        return carry

    lax.fori_loop(0, 2, deliver, 0)

    arrive(notes, recvs.at[6])
    lanes = lax.broadcasted_iota(i32, (1, 128), 1)
    total = jnp.sum(jnp.where(lanes == 32, jnp.sum(notes[...], axis=(0, 1)), 0.0), axis=1, keepdims=True)
    scale = jnp.minimum(1.0, 0.04 / (jnp.sqrt(total / (N * 32 * 8192)) + 1e-06))
    for copy in copies[3:]:
        copy.wait()

    for s in range(2):
        from_group = table[s, me] // RANKS
        for d in range(RANKS):
            tops = notes[d, from_group] * (scale / (LEVELS * LEVELS))
            column = jnp.sum(jnp.where(lane == row, tops, 0.0), axis=1, keepdims=True)
            factor[s, 32 * d:32 * d + 32] = jnp.broadcast_to(column, (32, 128))

    def compute(s, carry):
        arrive(land.at[s], recvs.at[2 + s])

        def decode(d, inner):
            rows = pl.ds(pl.multiple_of(64 * d, 64), 64)
            for j in range(4):
                cols = pl.ds(128 * j, 128)
                code = land[s, rows, cols].astype(i32).astype(f32)
                grad_s[s, 0, rows, cols], grad_s[s, 1, rows, cols] = split(code * jnp.abs(code) * factor[s, rows])
            return inner

        lax.fori_loop(0, ORDER // 64, decode, 0)
        lh, ll, rh, rl = basis_s[0, s, 0], basis_s[0, s, 1], basis_s[1, s, 0], basis_s[1, s, 1]
        half_turned = product((turned_s[0, s, 0], turned_s[0, s, 1]), (grad_s[s, 0], grad_s[s, 1]), ((1,), (0,)))
        work_s[0], work_s[1] = split(half_turned)
        turned = product((work_s[0], work_s[1]), (rh, rl), ((1,), (0,)))
        kept = table[2 + s, me] > 0
        moved = jnp.where(kept, 0.9, 1.0) * old_v[0, s] + jnp.where(kept, 0.1, 0.0) * turned
        spread = jnp.where(kept, 0.95, 1.0) * old_v[1, s] + jnp.where(kept, 0.05, 0.0) * turned * turned
        new_first[s] = moved
        new_second[s] = spread
        direction = moved * (1.0 / FIRST_CORRECTION) / (jnp.sqrt(spread * (1.0 / SECOND_CORRECTION)) + 1e-08)
        work_s[0], work_s[1] = split(direction)
        half_back = product((lh, ll), (work_s[0], work_s[1]), ((1,), (0,)))
        work_s[0], work_s[1] = split(half_back)
        update = product((work_s[0], work_s[1]), (turned_s[1, s, 0], turned_s[1, s, 1]), ((1,), (0,))).astype(bf16)
        for i in range(N):
            top_row, left_col = 32 * (i % RANKS) + 16 * (i // 64), 128 * (i // RANKS % 4)
            back[s, i] = update[top_row:top_row + 16, left_col:left_col + 128]
        mine = recv3.at[s * N + me]
        each_peer(me, lambda peer: remote(back.at[s, peer], mine, sends.at[3], recvs.at[4], peer))
        pltpu.make_async_copy(back.at[s, me], mine, recvs.at[4]).start()
        return carry

    lax.fori_loop(0, 2, compute, 0)

    def factors(s, carry):
        kept = table[2 + s, me] > 0
        stay, fresh = jnp.where(kept, 0.95, 1.0), jnp.where(kept, 0.05, 0.0)
        halves = (grad_s[s, 0], grad_s[s, 1])
        new_left[s] = stay * old_v[2, s] + fresh * product(halves, halves, ((1,), (1,)))
        new_right[s] = stay * old_v[3, s] + fresh * product(halves, halves, ((0,), (0,)))
        return carry

    lax.fori_loop(0, 2, factors, 0)

    arrive(recv3, recvs.at[4])

    def collect(g):
        for c in range(RANKS):
            send4[g, c] = recv3[table[4, RANKS * g + c]]

    for d in range(1, GROUPS):
        to = lax.rem(group + d, GROUPS)
        collect(to)
        remote(send4.at[to], recv4.at[group], sends.at[4], arrivals.at[d], to * RANKS + rank)
    collect(group)
    pltpu.make_async_copy(send4.at[group], recv4.at[group], arrivals.at[0]).start()
    for d in range(GROUPS):
        source = lax.rem(group + GROUPS - d, GROUPS)
        arrive(recv4.at[source], arrivals.at[d])
        source_row = pl.multiple_of(16 * (source // 4), 16)
        source_col = 128 * lax.rem(source, 4)
        for c in range(RANKS):
            col = pl.multiple_of(ORDER * c + source_col, 128)
            updates[pl.ds(source_row, 16), pl.ds(col, 128)] = recv4[source, c]
    others = pl.ds(0, N - 1)
    arrive(send1.at[pl.ds(0, GROUPS - 1)], sends.at[0])
    arrive(notes1.at[pl.ds(0, GROUPS - 1)], sends.at[1])
    arrive(notes.at[pl.ds(0, RANKS - 1)], sends.at[5])
    arrive(send4.at[pl.ds(0, GROUPS - 1)], sends.at[4])
    for s in range(2):
        arrive(send2.at[s, others], sends.at[2])
        arrive(recv3.at[others], sends.at[3])


def settle_kernel(*refs):
    count = len(refs) // 2
    copies = [pltpu.make_async_copy(refs[k], refs[count + k], refs[-1].at[k]) for k in range(count)]
    for copy in copies:
        copy.start()
    for copy in copies:
        copy.wait()


def per_device(grad, block_owner, left_factor, right_factor, left_basis, right_basis, first_moment, second_moment):
    state = pltpu.VMEM((2, ORDER, ORDER), f32)
    in_hbm = pl.BlockSpec(memory_space=pl.ANY)
    in_vmem = pl.BlockSpec(memory_space=pltpu.VMEM)
    results = pl.pallas_call(
        step_kernel,
        out_shape=[pltpu.VMEM(grad.shape, bf16)] + [state] * 4,
        in_specs=[in_vmem] + [in_hbm] * 7,
        out_specs=[in_vmem] * 5,
        scratch_shapes=[
            pltpu.VMEM((8, N), i32),
            pltpu.SMEM((8, N), i32),
            pltpu.VMEM((2, ORDER, 128), f32),
            pltpu.VMEM(grad.shape, f32),
            pltpu.VMEM((2, 2, ORDER, ORDER), f32),
            pltpu.VMEM((4, 2, ORDER, ORDER), f32),
            pltpu.VMEM((2, 2, 2, ORDER, ORDER), bf16),
            pltpu.VMEM((2, 2, 2, ORDER, ORDER), bf16),
            pltpu.VMEM((1, 128), f32),
            pltpu.VMEM((GROUPS, 1, 128), f32),
            pltpu.VMEM((RANKS, GROUPS, 1, 128), f32),
            pltpu.VMEM((32, 128), f32),
            pltpu.VMEM((GROUPS, RANKS, 16, 128), i16),
            pltpu.VMEM((N, 16, 128), i16),
            pltpu.VMEM((2, N, 16, 128), i16),
            pltpu.VMEM((2, ORDER, ORDER), i16),
            pltpu.VMEM((2, 2, ORDER, ORDER), bf16),
            pltpu.VMEM((2, ORDER, ORDER), bf16),
            pltpu.VMEM((2, N, 16, 128), bf16),
            pltpu.VMEM((2 * N, 16, 128), bf16),
            pltpu.VMEM((GROUPS, RANKS, 16, 128), bf16),
            pltpu.VMEM((GROUPS, RANKS, 16, 128), bf16),
            pltpu.SemaphoreType.DMA((8,)),
            pltpu.SemaphoreType.DMA((6,)),
            pltpu.SemaphoreType.DMA((7,)),
            pltpu.SemaphoreType.DMA((GROUPS,)),
            pltpu.SemaphoreType.REGULAR,
        ],
        compiler_params=pltpu.CompilerParams(
            collective_id=0, has_side_effects=True, vmem_limit_bytes=50 * 2**20),
        name="soap_step",
    )(block_owner.reshape(1, N), grad, left_basis, right_basis, first_moment, second_moment, left_factor, right_factor)
    return pl.pallas_call(
        settle_kernel,
        out_shape=[jax.ShapeDtypeStruct(r.shape, r.dtype) for r in results],
        in_specs=[in_hbm] * 5,
        out_specs=[in_hbm] * 5,
        scratch_shapes=[pltpu.SemaphoreType.DMA((5,))],
        compiler_params=pltpu.CompilerParams(vmem_limit_bytes=2**20),
        name="settle",
    )(*results)


def solution(mesh):
    rows, state = P("dp", None), P("dp", None, None)
    return jax.shard_map(
        per_device, mesh=mesh, in_specs=(rows, P()) + (state,) * 6,
        out_specs=(rows,) + (state,) * 4, check_vma=False,
    )
```
